32 devices in a mesh: dp: 4 (over z), vocab: 8 (over y, x, core).
Axes of the slice: x: 2, y: 2, z: 4, core: 2. Of those that a mesh axis runs over, the one named last changes fastest.
Arguments:
- tokens_in: bfloat16 [512, 8192], P('dp'), may hold values from -80 to 80
- gain: float32 [8192], replicated, may hold values from 0.5 to 1.5
- head_weight: bfloat16 [8192, 16896], P(None, 'vocab'), may hold values from -0.5 to 0.5
- teacher_ids: int32 [512, 16], P('dp'), may hold values from 0 to 16895
- teacher_weight: float32 [512, 16], P('dp'), may hold values from 0.05 to 1
- labels: int32 [512], P('dp'), may hold values from 0 to 16895
Outputs:
- token_loss: float32 [512], P('dp')
- grad_input: bfloat16 [512, 8192], P('dp', 'vocab')
- head_grad: float32 [2112, 8, 8192], P('dp', 'vocab')
The draws below stay inside these ranges and needn't reach their ends.
All inputs are finite; a program needn't handle non-finite values.
Results may differ from the reference program's by a relative error of at most 0.015.
Values may be sent and summed in bfloat16 or wider, within the bound.
A program may use at most 192 MiB of HBM per device.

```python
import math
import jax
import jax.numpy as jnp
import numpy as np
from jax import lax

D = 8192
V = 16896
TOPK = 16
TOK_DEV = 128
TOKENS = 512
N_DP = 4
N_VOCAB = 8


def pair_vectors(key):
    strength = jnp.array([120.0, 160.0, 200.0, 250.0], jnp.float32)
    noise = jnp.clip(jax.random.normal(jax.random.fold_in(key, 7), (4, D), jnp.float32), -3.0, 3.0)
    return (noise, strength)


def draw_head_weight(key, part):
    base = jax.random.normal(jax.random.fold_in(key, 1), (D, V), jnp.float32) * (3.0 / math.sqrt(D))
    base = jnp.clip(base, -0.25, 0.25)
    noise, strength = pair_vectors(key)
    aligned = noise * (strength[:, None] / D)
    shrink = 1.0 - 2.0 / strength
    columns = jnp.arange(4, dtype=jnp.int32) * (V // 4) + 5
    base = base.at[:, columns].set(jnp.transpose(aligned))
    base = base.at[:, columns + 1].set(jnp.transpose(aligned * shrink[:, None]))
    return base.astype(jnp.bfloat16)


def draw_tokens_in(key, part):
    noise = jax.random.normal(jax.random.fold_in(key, 2), (TOKENS, D), jnp.float32)
    row_scales = jnp.exp(jax.random.uniform(jax.random.fold_in(key, 3), (TOKENS,), jnp.float32, 0.0, math.log(10.0)))
    col_scales = jnp.exp(jax.random.uniform(jax.random.fold_in(key, 5), (D,), jnp.float32, 0.0, math.log(10.0)))
    values = noise * row_scales[:, None] * col_scales[None, :]
    pair_noise, strength = pair_vectors(key)
    chosen = jnp.arange(4, dtype=jnp.int32) * (TOKENS // 4) + 3
    values = values.at[chosen].set(pair_noise * 10.0)
    return jnp.clip(values, -80.0, 80.0).astype(jnp.bfloat16)


def touch_ends(values, own_key, least, high):
    index_at = [jax.random.randint(jax.random.fold_in(own_key, axis), (), 0, length) for axis, length in enumerate(values.shape)]
    main_axis = values.shape.index(max(values.shape))
    next_to = index_at[:main_axis] + [(index_at[main_axis] + 1) % values.shape[main_axis]] + index_at[main_axis + 1:]
    return values.at[tuple(index_at)].set(least).at[tuple(next_to)].set(high)


def level_of(rng, shape, split, least, largest):
    loudness, own = 1.0, jax.random.fold_in(rng, 6)
    for dim, parts in split:
        heights = jnp.exp(jax.random.uniform(jax.random.fold_in(own, dim), (parts,), jnp.float32, least / len(split), largest / len(split)))
        loudness = loudness * jnp.repeat(heights, shape[dim] // parts).reshape([-1 if axis == dim else 1 for axis in range(len(shape))])
    return loudness


def cumulative_ranks(amount, skew):
    loads = [(1 << 20) // math.isqrt(rank ** skew) + 1 for rank in range(1, amount + 1)]
    scale = 1 + sum(loads) // (1 << 30)
    return np.cumsum(np.array([max(1, weight // scale) for weight in loads]))


def ranked_ids(key, extent, amount, lean):
    listing = cumulative_ranks(amount, lean)
    lot = jax.random.randint(jax.random.fold_in(key, 1), extent, 0, int(listing[amount - 1]))
    grade = jnp.searchsorted(jnp.asarray(listing, jnp.int32), lot, side="right")
    return jax.random.permutation(jax.random.fold_in(key, 2), amount)[grade].astype(jnp.int32)


def setup_inputs(seed: int = 0) -> dict:
    key_list = jax.random.split(jax.random.key(seed), 7)
    tokens_in = draw_tokens_in(jax.random.fold_in(key_list[6], 71), 0)
    gain = jnp.clip(1.0 + 0.1 * jax.random.normal(key_list[1], (D,), jnp.float32), 0.5, 1.5)
    head_weight = draw_head_weight(jax.random.fold_in(key_list[6], 71), 0)
    teacher_ids = touch_ends(ranked_ids(key_list[3], (TOKENS, TOPK), V, 2), jax.random.fold_in(key_list[3], 3), 0, V - 1).astype(jnp.int32)
    teacher_weight = jnp.clip(jnp.exp(math.log(1.0) - 2.9957323 * jax.random.uniform(key_list[4], (TOKENS, TOPK), jnp.float32) ** level_of(key_list[4], (TOKENS, TOPK), ((0, 4),), -0.2, 0.2)), 0.05, 1.0)
    labels = touch_ends(ranked_ids(key_list[5], (TOKENS,), V, 2), jax.random.fold_in(key_list[5], 3), 0, V - 1).astype(jnp.int32)
    return dict(tokens_in=tokens_in, gain=gain, head_weight=head_weight, teacher_ids=teacher_ids, teacher_weight=teacher_weight, labels=labels)


LABEL_SHARE = 0.5
EPS = 1e-05

def normalize(tokens_in, gain):
    as_float = tokens_in.astype(jnp.float32)
    row_scale = jnp.sqrt(lax.optimization_barrier(jnp.mean(as_float * as_float, axis=1, keepdims=True)) + EPS)
    normed = (as_float / row_scale * gain[None, :]).astype(jnp.bfloat16)
    return (as_float, row_scale, normed)

def targets(teacher_ids, teacher_probs, labels, col_start, col_width):
    columns = col_start + jnp.arange(col_width, dtype=jnp.int32)
    matches = (teacher_ids[:, :, None] == columns[None, None, :]).astype(jnp.float32)
    teacher_part = lax.optimization_barrier(jnp.sum(teacher_probs[:, :, None] * matches, axis=1))
    label_part = (labels[:, None] == columns[None, :]).astype(jnp.float32)
    return (1.0 - LABEL_SHARE) * teacher_part + LABEL_SHARE * label_part

def round_half(values):
    return lax.optimization_barrier(values.astype(jnp.bfloat16)).astype(jnp.float32)

def reference(tokens_in, gain, head_weight, teacher_ids, teacher_weight, labels):
    as_float, row_scale, normed = normalize(tokens_in, gain)
    logits = jnp.dot(normed, head_weight, preferred_element_type=jnp.float32)
    teacher_probs = teacher_weight / lax.optimization_barrier(jnp.sum(teacher_weight, axis=1, keepdims=True))
    col_width = V // N_VOCAB

    def one_block(block_index):
        return targets(teacher_ids, teacher_probs, labels, (block_index * col_width).astype(jnp.int32), col_width)
    blocks = lax.map(one_block, jnp.arange(N_VOCAB, dtype=jnp.int32))
    target = jnp.transpose(blocks, (1, 0, 2)).reshape(TOKENS, V)
    row_top = lax.optimization_barrier(jnp.max(logits, axis=1))
    total_exp = lax.optimization_barrier(jnp.sum(jnp.exp(logits - row_top[:, None]), axis=1))
    total_dot = lax.optimization_barrier(jnp.sum(target * logits, axis=1))
    lse = row_top + jnp.log(total_exp)
    token_loss = (1.0 - LABEL_SHARE) * lax.optimization_barrier(jnp.sum(teacher_probs * jnp.log(teacher_probs), axis=1)) - total_dot + lse
    dlogits = (jnp.exp(logits - lse[:, None]) - target).astype(jnp.bfloat16)

    def add_block(block_index, running):
        first = (block_index * col_width).astype(jnp.int32)
        grad_block = lax.dynamic_slice_in_dim(dlogits, first, col_width, 1)
        weight_block = lax.dynamic_slice_in_dim(head_weight, first, col_width, 1)
        partial_value = lax.dot_general(grad_block, weight_block, (((1,), (1,)), ((), ())), preferred_element_type=jnp.float32)
        return running + round_half(partial_value)
    dhidden = lax.fori_loop(0, N_VOCAB, add_block, jnp.zeros((TOKENS, D), jnp.float32))
    scaled = dhidden * gain[None, :]
    inner_sum = lax.optimization_barrier(jnp.sum(scaled * as_float, axis=1, keepdims=True))
    grad_input = (scaled / row_scale - as_float * inner_sum / (D * row_scale * row_scale * row_scale)).astype(jnp.bfloat16)

    def add_replica(replica, running):
        first = (replica * TOK_DEV).astype(jnp.int32)
        grad_block = lax.dynamic_slice_in_dim(dlogits, first, TOK_DEV, 0)
        normed_block = lax.dynamic_slice_in_dim(normed, first, TOK_DEV, 0)
        partial_value = lax.dot_general(grad_block, normed_block, (((0,), (0,)), ((), ())), preferred_element_type=jnp.float32)
        return running + round_half(partial_value)
    head_total = lax.fori_loop(0, N_DP, add_replica, jnp.zeros((V, D), jnp.float32))
    head_grad = jnp.transpose(head_total.reshape(N_VOCAB, col_width, D), (1, 0, 2))
    return (token_loss, grad_input, head_grad)
```

```python
import jax
import jax.numpy as jnp
from jax import lax
from jax.sharding import PartitionSpec as P

LABEL_SHARE = 0.5
EPS = 1e-05


def normalize(tokens_in, gain):
    as_float = tokens_in.astype(jnp.float32)
    row_scale = jnp.sqrt(jnp.mean(as_float * as_float, axis=1, keepdims=True) + EPS)
    normed = (as_float / row_scale * gain[None, :]).astype(jnp.bfloat16)
    return (as_float, row_scale, normed)


def targets(teacher_ids, teacher_probs, labels, col_start, col_width):
    columns = col_start + jnp.arange(col_width, dtype=jnp.int32)
    matches = (teacher_ids[:, :, None] == columns[None, None, :]).astype(jnp.float32)
    teacher_part = jnp.sum(teacher_probs[:, :, None] * matches, axis=1)
    label_part = (labels[:, None] == columns[None, :]).astype(jnp.float32)
    return (1.0 - LABEL_SHARE) * teacher_part + LABEL_SHARE * label_part


def local(tokens_in, gain, head_weight, teacher_ids, teacher_weight, labels):
    features, col_width = head_weight.shape
    slice_width = features // lax.axis_size("vocab")
    here = lax.axis_index("vocab")
    col_start = here * col_width
    slice_start = here * slice_width
    local_tokens = lax.dynamic_slice_in_dim(tokens_in, slice_start, slice_width, 1)
    mine = lax.all_gather(local_tokens, "dp", axis=0, tiled=True)
    everyone = lax.all_gather(mine, "vocab", axis=1, tiled=True)

    as_float, row_scale, normed = normalize(tokens_in, gain)
    logits = jnp.dot(normed, head_weight, preferred_element_type=jnp.float32)
    teacher_probs = teacher_weight / jnp.sum(teacher_weight, axis=1, keepdims=True)
    target = targets(teacher_ids, teacher_probs, labels, col_start, col_width)
    local_dot = jnp.sum(target * logits, axis=1)
    local_top = jnp.max(logits, axis=1)
    expo = jnp.exp(logits - local_top[:, None])
    stats = jnp.stack([local_top, jnp.sum(expo, axis=1), local_dot, jnp.sum(expo * logits, axis=1)])
    stats = lax.all_gather(stats, "vocab", axis=0)
    row_top = jnp.max(stats[:, 0], axis=0)
    shrink = jnp.exp(stats[:, 0] - row_top[None, :])
    total_exp = jnp.sum(stats[:, 1] * shrink, axis=0)
    total_dot = jnp.sum(stats[:, 2], axis=0)
    mean_logit = jnp.sum(stats[:, 3] * shrink, axis=0) / total_exp
    lse = row_top + jnp.log(total_exp)
    token_loss = (
        (1.0 - LABEL_SHARE) * jnp.sum(teacher_probs * jnp.log(teacher_probs), axis=1)
        - total_dot
        + lse
    )
    dlogits = (jnp.exp(logits - lse[:, None]) - target).astype(jnp.bfloat16)
    all_dlogits = lax.all_to_all(dlogits, "dp", split_axis=1, concat_axis=0, tiled=True)

    partial_value = lax.dot_general(
        dlogits, head_weight, (((1,), (1,)), ((), ())), preferred_element_type=jnp.float32
    )
    dhidden = lax.psum_scatter(
        partial_value.astype(jnp.bfloat16), "vocab", scatter_dimension=1, tiled=True
    ).astype(jnp.float32)
    local_gain = lax.dynamic_slice_in_dim(gain, slice_start, slice_width, 0)
    scaled = dhidden * local_gain[None, :]
    inner_over_scale = (mean_logit - total_dot)[:, None]
    grad_input = (
        scaled / row_scale
        - local_tokens.astype(jnp.float32) * inner_over_scale / (features * row_scale * row_scale)
    ).astype(jnp.bfloat16)

    _, _, all_normed = normalize(everyone, gain)
    head_grad = lax.dot_general(
        all_dlogits, all_normed, (((0,), (0,)), ((), ())), preferred_element_type=jnp.float32
    )
    return (token_loss, grad_input, head_grad[:, None, :])


def solution(mesh):
    in_specs = (P("dp", None), P(), P(None, "vocab"), P("dp", None), P("dp", None), P("dp"))
    out_specs = (P("dp"), P("dp", "vocab"), P("dp", "vocab", None))
    return jax.shard_map(local, mesh=mesh, in_specs=in_specs, out_specs=out_specs, check_vma=False)
```

```python
import functools

import jax
import jax.numpy as jnp
from jax import lax
from jax.experimental import pallas as pl
from jax.experimental.pallas import tpu as pltpu
from jax.sharding import PartitionSpec as P

LABEL_SHARE = 0.5
EPS = 1e-05


def normalize(tokens_in, gain):
    as_float = tokens_in.astype(jnp.float32)
    row_scale = jnp.sqrt(jnp.mean(as_float * as_float, axis=1, keepdims=True) + EPS)
    normed = (as_float / row_scale * gain[None, :]).astype(jnp.bfloat16)
    return (as_float, row_scale, normed)


def targets(teacher_ids, teacher_probs, labels, col_start, col_width):
    columns = col_start + jnp.arange(col_width, dtype=jnp.int32)
    matches = (teacher_ids[:, :, None] == columns[None, None, :]).astype(jnp.float32)
    teacher_part = jnp.sum(teacher_probs[:, :, None] * matches, axis=1)
    label_part = (labels[:, None] == columns[None, :]).astype(jnp.float32)
    return (1.0 - LABEL_SHARE) * teacher_part + LABEL_SHARE * label_part


def local(tokens_in, gain, head_weight, teacher_ids, teacher_weight, labels):
    features, col_width = head_weight.shape
    slice_width = features // lax.axis_size("vocab")
    here = lax.axis_index("vocab")
    col_start = here * col_width
    slice_start = here * slice_width
    local_tokens = lax.dynamic_slice_in_dim(tokens_in, slice_start, slice_width, 1)
    mine = lax.all_gather(local_tokens, "dp", axis=0, tiled=True)
    everyone = lax.all_gather(mine, "vocab", axis=1, tiled=True)

    as_float, row_scale, normed = normalize(tokens_in, gain)
    logits = jnp.dot(normed, head_weight, preferred_element_type=jnp.float32)
    teacher_probs = teacher_weight / jnp.sum(teacher_weight, axis=1, keepdims=True)
    target = targets(teacher_ids, teacher_probs, labels, col_start, col_width)
    local_dot = jnp.sum(target * logits, axis=1)
    local_top = jnp.max(logits, axis=1)
    expo = jnp.exp(logits - local_top[:, None])
    stats = jnp.stack([local_top, jnp.sum(expo, axis=1), local_dot, jnp.sum(expo * logits, axis=1)])
    stats = lax.all_gather(stats, "vocab", axis=0)
    row_top = jnp.max(stats[:, 0], axis=0)
    shrink = jnp.exp(stats[:, 0] - row_top[None, :])
    total_exp = jnp.sum(stats[:, 1] * shrink, axis=0)
    total_dot = jnp.sum(stats[:, 2], axis=0)
    mean_logit = jnp.sum(stats[:, 3] * shrink, axis=0) / total_exp
    lse = row_top + jnp.log(total_exp)
    token_loss = (
        (1.0 - LABEL_SHARE) * jnp.sum(teacher_probs * jnp.log(teacher_probs), axis=1)
        - total_dot
        + lse
    )
    dlogits = (jnp.exp(logits - lse[:, None]) - target).astype(jnp.bfloat16)
    all_dlogits = lax.all_to_all(dlogits, "dp", split_axis=1, concat_axis=0, tiled=True)

    partial_value = lax.dot_general(
        dlogits, head_weight, (((1,), (1,)), ((), ())), preferred_element_type=jnp.float32
    )
    dhidden = lax.psum_scatter(
        partial_value.astype(jnp.bfloat16), "vocab", scatter_dimension=1, tiled=True
    ).astype(jnp.float32)
    local_gain = lax.dynamic_slice_in_dim(gain, slice_start, slice_width, 0)
    scaled = dhidden * local_gain[None, :]
    inner_over_scale = (mean_logit - total_dot)[:, None]
    grad_input = (
        scaled / row_scale
        - local_tokens.astype(jnp.float32) * inner_over_scale / (features * row_scale * row_scale)
    ).astype(jnp.bfloat16)

    _, _, all_normed = normalize(everyone, gain)
    head_grad = lax.dot_general(
        all_dlogits, all_normed, (((0,), (0,)), ((), ())), preferred_element_type=jnp.float32
    )
    return (token_loss, grad_input, head_grad[:, None, :])


MESH = pl.DeviceIdType.MESH
VMEM_BYTES = 60 * 1024 * 1024


def fused_kernel(
    nz, nv,
    normed, xs, gs, rs, target, entropy, w_hbm,
    loss_o, gin_o, gath_o, dlt_o,
    w_v, logits_v, dl_v, dlt_v, scol, stat_s, stat_r, send_p, recv_p, own, send_c, recv_c,
    w_sem, z_send, z_recv, f_send, f_recv, k_send, k_recv, st_send, st_recv,
    d_send, d_recv, p_send, p_recv, c_send, c_recv, loc_sem,
):
    tok, features = normed.shape
    cols = w_hbm.shape[1]
    nc = nv // 2
    slw = features // nv
    half = features // 2
    share = cols // nz
    z = lax.axis_index("dp")
    p = lax.axis_index("vocab")
    chip, core = p // 2, p % 2
    partner = chip * 2 + (1 - core)

    def chip_at(step):
        return lax.rem(chip + step, nc)

    def z_at(step):
        return lax.rem(z + step, nz)

    barrier = pltpu.get_barrier_semaphore()
    for r in range(1, nz):
        pl.semaphore_signal(barrier, inc=1, device_id={"dp": z_at(r)}, device_id_type=MESH)
    for r in range(1, nv):
        pl.semaphore_signal(
            barrier, inc=1, device_id={"vocab": lax.rem(p + r, nv)}, device_id_type=MESH
        )

    chunk = 512
    n_chunks = features // chunk

    def w_copy(k):
        rows = pl.ds(pl.multiple_of(k * chunk, chunk), chunk)
        return pltpu.make_async_copy(w_hbm.at[rows, :], w_v.at[rows, :], w_sem.at[k])

    @pl.loop(0, n_chunks)
    def _(k):
        w_copy(k).start()

    pl.semaphore_wait(barrier, nz - 1 + nv - 1)

    def rows_of(zz):
        return pl.ds(pl.multiple_of(zz * tok, tok), tok)

    def slice_of(c, k):
        return pl.ds(pl.multiple_of((k * nc + c) * slw, slw), slw)

    def half_of(k):
        return pl.ds(pl.multiple_of(k * half, half), half)

    def z_copy(r):
        return pltpu.make_async_remote_copy(
            normed.at[:, slice_of(chip, core)],
            gath_o.at[rows_of(z), slice_of(chip, core)],
            z_send.at[r], z_recv.at[r], device_id={"dp": z_at(r)}, device_id_type=MESH,
        )

    def f_copy(r, step):
        region = gath_o.at[rows_of(z_at(nz - r)), slice_of(chip, core)]
        return pltpu.make_async_remote_copy(
            region, region, f_send.at[r, step], f_recv.at[r, step],
            device_id={"vocab": chip_at(step) * 2 + core}, device_id_type=MESH,
        )

    def k_copy(r):
        region = gath_o.at[rows_of(z_at(nz - r)), half_of(core)]
        return pltpu.make_async_remote_copy(
            region, region, k_send.at[r], k_recv.at[r],
            device_id={"vocab": partner}, device_id_type=MESH,
        )

    order = sorted(range(1, nz), key=lambda r: (min(r, nz - r), r))

    def forward(r):
        z_copy(r).wait_recv()
        for step in range(1, nc):
            f_copy(r, step).start()

    def forward_core(r):
        for step in range(1, nc):
            f_copy(r, step).wait_recv()
        k_copy(r).start()

    for r in order:
        z_copy(r).start()
    mine = pltpu.make_async_copy(normed, gath_o.at[rows_of(z), :], loc_sem.at[0])
    mine.start()

    logits_v[...] = jnp.zeros_like(logits_v)

    def logit_chunk(k):
        w_copy(k).wait()
        rows = pl.ds(pl.multiple_of(k * chunk, chunk), chunk)
        logits_v[:, :cols] += jnp.dot(
            normed[:, rows], w_v[rows, :], preferred_element_type=jnp.float32
        )

    pl.loop(0, n_chunks // 2)(logit_chunk)
    forward(order[0])
    pl.loop(n_chunks // 2, n_chunks)(logit_chunk)

    group = 16

    @pl.loop(0, tok // group)
    def _(g):
        rows = pl.ds(pl.multiple_of(g * group, group), group)
        lg = logits_v[rows, :cols]
        top = jnp.max(lg, axis=1, keepdims=True)
        expo = jnp.exp(lg - top)
        lane = lax.broadcasted_iota(jnp.int32, (group, 128), 1)
        total = jnp.sum(expo, axis=1, keepdims=True)
        dot = jnp.sum(target[rows, :] * lg, axis=1, keepdims=True)
        weighted = jnp.sum(expo * lg, axis=1, keepdims=True)
        scol[rows, :] = jnp.where(
            lane == 0, top, jnp.where(lane == 1, total, jnp.where(lane == 2, dot, weighted))
        )

    stat_s[...] = jnp.transpose(scol[...])[:8]

    def st_copy(r):
        return pltpu.make_async_remote_copy(
            stat_s, stat_r.at[r], st_send.at[r], st_recv.at[r],
            device_id={"vocab": lax.rem(p + r, nv)}, device_id_type=MESH,
        )

    for r in range(1, nv):
        st_copy(r).start()
    for r in order[1:2]:
        forward(r)
    for r in range(1, nv):
        st_copy(r).wait_recv()
    stats = [stat_s[...]] + [stat_r[r] for r in range(1, nv)]
    row_top = functools.reduce(jnp.maximum, [s[0:1] for s in stats])
    shrink = [jnp.exp(s[0:1] - row_top) for s in stats]
    total_exp = sum(s[1:2] * f for s, f in zip(stats, shrink))
    total_dot = sum(s[2:3] for s in stats)
    mean_logit = sum(s[3:4] * f for s, f in zip(stats, shrink)) / total_exp
    lse = row_top + jnp.log(total_exp)
    loss_o[...] = entropy[...] - total_dot + lse
    sub = lax.broadcasted_iota(jnp.int32, (tok, tok), 0)
    back = jnp.where(sub == 0, lse, mean_logit - total_dot)
    scol[...] = jnp.transpose(back)

    @pl.loop(0, tok // group)
    def _(g):
        rows = pl.ds(pl.multiple_of(g * group, group), group)
        dl = jnp.exp(logits_v[rows, :cols] - scol[rows, 0:1]) - target[rows, :]
        logits_v[rows, :cols] = dl
        dl_v[rows, :] = dl.astype(jnp.bfloat16)

    for c in range((cols + 127) // 128):
        size = min(128, cols - c * 128)
        block = jnp.transpose(logits_v[:, c * 128:(c + 1) * 128])
        dlt_v[c * 128:c * 128 + size, :] = block[:size].astype(jnp.bfloat16)

    def share_of(zz):
        return pl.ds(pl.multiple_of(zz * share, 16), share)

    def d_copy(r):
        return pltpu.make_async_remote_copy(
            dlt_v.at[share_of(z_at(r)), :], dlt_o.at[:, rows_of(z)],
            d_send.at[r], d_recv.at[r], device_id={"dp": z_at(r)}, device_id_type=MESH,
        )

    for r in order:
        d_copy(r).start()
    mine_d = pltpu.make_async_copy(dlt_v.at[share_of(z), :], dlt_o.at[:, rows_of(z)], loc_sem.at[1])
    mine_d.start()
    for r in order[2:]:
        forward(r)

    def p_copy(step):
        return pltpu.make_async_remote_copy(
            send_p.at[step], recv_p.at[step], p_send.at[step], p_recv.at[step],
            device_id={"vocab": partner}, device_id_type=MESH,
        )

    def c_copy(step):
        return pltpu.make_async_remote_copy(
            send_c.at[step], recv_c.at[step], c_send.at[step], c_recv.at[step],
            device_id={"vocab": chip_at(step) * 2 + core}, device_id_type=MESH,
        )

    tile = 256

    def product(step, which, dest):
        start = (chip_at(step) * 2 + which) * slw

        @pl.loop(0, slw // tile)
        def _(j):
            rows = pl.ds(pl.multiple_of(start + j * tile, tile), tile)
            here = pl.ds(pl.multiple_of(j * tile, tile), tile)
            dest[step, :, here] = lax.dot_general(
                dl_v[...], w_v[rows, :], (((1,), (1,)), ((), ())),
                preferred_element_type=jnp.float32,
            ).astype(dest.dtype)

    def pass_on(step):
        p_copy(step).wait_recv()
        send_c[step] = (own[step] + recv_p[step].astype(jnp.float32)).astype(jnp.bfloat16)
        c_copy(step).start()

    steps = list(range(1, nc)) + [0]
    for at, step in enumerate(steps):
        product(step, 1 - core, send_p)
        p_copy(step).start()
        product(step, core, own)
        if at > 0:
            pass_on(steps[at - 1])

    for r in order:
        forward_core(r)
    p_copy(0).wait_recv()
    for step in range(1, nc):
        c_copy(step).wait_recv()

    @pl.loop(0, tok // group)
    def _(g):
        rows = pl.ds(pl.multiple_of(g * group, group), group)
        dh = own[0, rows, :] + recv_p[0, rows, :].astype(jnp.float32)
        for step in range(1, nc):
            dh += recv_c[step, rows, :].astype(jnp.float32)
        scale = rs[rows, 0:1]
        inner = scol[rows, 1:2] / (features * scale * scale)
        gin_o[rows, :] = (
            dh * gs[...] / scale - xs[rows, :].astype(jnp.float32) * inner
        ).astype(jnp.bfloat16)

    for r in order:
        k_copy(r).wait()
        d_copy(r).wait()
        z_copy(r).wait_send()
        for step in range(1, nc):
            f_copy(r, step).wait_send()
    for r in range(1, nv):
        st_copy(r).wait_send()
    for step in range(nc):
        p_copy(step).wait_send()
    for step in range(1, nc):
        c_copy(step).wait_send()
    mine.wait()
    mine_d.wait()


def head_kernel(a_ref, n_ref, out_ref):
    out_ref[:, 0, :] = jnp.dot(a_ref[...], n_ref[...], preferred_element_type=jnp.float32)


def local_fused(nz, nv, tokens_in, gain, head_weight, teacher_ids, teacher_weight, labels):
    features, cols = head_weight.shape
    tok = tokens_in.shape[0]
    slw, share, nc = features // nv, cols // nz, nv // 2
    here = lax.axis_index("vocab")
    _, row_scale, normed = normalize(tokens_in, gain)
    teacher_probs = teacher_weight / jnp.sum(teacher_weight, axis=1, keepdims=True)
    target = targets(teacher_ids, teacher_probs, labels, here * cols, cols)
    entropy = (1.0 - LABEL_SHARE) * jnp.sum(teacher_probs * jnp.log(teacher_probs), axis=1)
    xs = lax.dynamic_slice_in_dim(tokens_in, here * slw, slw, 1)
    gs = lax.dynamic_slice_in_dim(gain, here * slw, slw, 0)
    vmem = pl.BlockSpec(memory_space=pltpu.VMEM)
    hbm = pl.BlockSpec(memory_space=pl.ANY)
    dma = pltpu.SemaphoreType.DMA
    loss, grad_input, gathered, dlt = pl.pallas_call(
        functools.partial(fused_kernel, nz, nv),
        out_shape=(
            jax.ShapeDtypeStruct((1, tok), jnp.float32),
            jax.ShapeDtypeStruct((tok, slw), jnp.bfloat16),
            jax.ShapeDtypeStruct((nz * tok, features), jnp.bfloat16),
            jax.ShapeDtypeStruct((share, nz * tok), jnp.bfloat16),
        ),
        in_specs=[vmem] * 6 + [hbm],
        out_specs=(vmem, vmem, hbm, hbm),
        scratch_shapes=[
            pltpu.VMEM((features, cols), jnp.bfloat16),
            pltpu.VMEM((tok, (cols + 127) // 128 * 128), jnp.float32),
            pltpu.VMEM((tok, cols), jnp.bfloat16),
            pltpu.VMEM((cols, tok), jnp.bfloat16),
            pltpu.VMEM((tok, 128), jnp.float32),
            pltpu.VMEM((8, tok), jnp.float32),
            pltpu.VMEM((nv, 8, tok), jnp.float32),
            pltpu.VMEM((nc, tok, slw), jnp.bfloat16),
            pltpu.VMEM((nc, tok, slw), jnp.bfloat16),
            pltpu.VMEM((nc, tok, slw), jnp.float32),
            pltpu.VMEM((nc, tok, slw), jnp.bfloat16),
            pltpu.VMEM((nc, tok, slw), jnp.bfloat16),
            dma((features // 512,)),
            dma((nz,)), dma((nz,)), dma((nz, nc)), dma((nz, nc)), dma((nz,)), dma((nz,)),
            dma((nv,)), dma((nv,)), dma((nz,)), dma((nz,)),
            dma((nc,)), dma((nc,)), dma((nc,)), dma((nc,)), dma((2,)),
        ],
        compiler_params=pltpu.CompilerParams(
            collective_id=0, has_side_effects=True, vmem_limit_bytes=VMEM_BYTES
        ),
        name="fused",
    )(normed, xs, gs[None, :], row_scale, target, entropy[None, :], head_weight)

    width = 1024
    head_grad = pl.pallas_call(
        head_kernel,
        grid=(features // width,),
        out_shape=jax.ShapeDtypeStruct((share, 1, features), jnp.float32),
        in_specs=[
            pl.BlockSpec((share, nz * tok), lambda j: (0, 0)),
            pl.BlockSpec((nz * tok, width), lambda j: (0, j)),
        ],
        out_specs=pl.BlockSpec((share, 1, width), lambda j: (0, 0, j)),
        compiler_params=pltpu.CompilerParams(vmem_limit_bytes=VMEM_BYTES),
        name="head",
    )(dlt, gathered)
    return (loss[0], grad_input, head_grad)


def solution(mesh):
    nz, nv = mesh.shape["dp"], mesh.shape["vocab"]

    def choose(tokens_in, gain, head_weight, *rest):
        tok, (features, cols) = tokens_in.shape[0], head_weight.shape
        aligned = (
            tok == 128 and nv % 2 == 0 and features % (nv * 256) == 0 and cols % (nz * 16) == 0
        )
        fits = nz * tok * features <= 1 << 23 and features * cols <= 1 << 25
        if aligned and fits:
            return local_fused(nz, nv, tokens_in, gain, head_weight, *rest)
        return local(tokens_in, gain, head_weight, *rest)

    in_specs = (P("dp", None), P(), P(None, "vocab"), P("dp", None), P("dp", None), P("dp"))
    out_specs = (P("dp"), P("dp", "vocab"), P("dp", "vocab", None))
    return jax.shard_map(choose, mesh=mesh, in_specs=in_specs, out_specs=out_specs, check_vma=False)
```
